32 devices in a mesh: replica: 8 (over y, x, core), fsdp: 4 (over z).
Axes of the slice: x: 2, y: 2, z: 4, core: 2. Of those that a mesh axis runs over, the one named last changes fastest.
Arguments:
- inputs: bfloat16 [8, 1024, 8192], P('replica', 'fsdp'), may hold values from -6 to 6
- cotangent: bfloat16 [8, 1024, 512], P('replica', 'fsdp'), may hold values from -6 to 6
- weight: bfloat16 [8, 8192, 512], P('replica', 'fsdp'), may hold values from -0.0625 to 0.0625
- adam_first: bfloat16 [8, 8192, 512], P('replica', 'fsdp'), may hold values from -0.1875 to 0.1875
- adam_second: bfloat16 [8, 8192, 512], P('replica', 'fsdp'), may hold values from 0.00024414062 to 0.00390625
- outer_frag: bfloat16 [32, 8192], P('fsdp'), may hold values from -6 to 6
- local_frag: bfloat16 [8, 32, 8192], P('replica', 'fsdp'), may hold values from -6 to 6
- momentum: float32 [32, 8192], P('fsdp'), may hold values from -3 to 3
Outputs:
- input_grad: bfloat16 [8, 1024, 8192], P('replica', 'fsdp')
- new_weight: bfloat16 [8, 8192, 512], P('replica', 'fsdp')
- new_first: bfloat16 [8, 8192, 512], P('replica', 'fsdp')
- new_second: bfloat16 [8, 8192, 512], P('replica', 'fsdp')
- new_outer: float32 [32, 8192], P('fsdp')
- new_momentum: float32 [32, 8192], P('fsdp')
The draws below stay inside these ranges and needn't reach their ends.
All inputs are finite; a program needn't handle non-finite values.
Results may differ from the reference program's by a relative error of at most 0.0035.
Values may be sent and summed in bfloat16 or wider, within the bound.
A program may use at most 128 MiB of HBM per device.

```python
import math
import jax
import jax.numpy as jnp
from jax import lax

D = 8192
KVW = 512
TOK_DEV = 256
TOK_REP = 1024
REPLICAS = 8
FRAG_ROWS = 32
N_REPLICA = 8
N_FSDP = 4


def spiked(entries, stream_key, source, target, blocks, factor):
    owner, partner = [(jnp.arange(entries.shape[position]) // (entries.shape[position] // blocks)).reshape([-1 if axis == position else 1 for axis in range(entries.ndim)]) for position in (source, target)]
    chosen = jax.random.permutation(stream_key, blocks)[partner]
    strong = (owner == chosen) | (owner == (partner + blocks // 2) % blocks)
    return jnp.where(strong, factor * entries, entries)


def block_levels(own_key, shape, shards, smallest, high):
    level = 1.0
    for axis_at, blocks in shards:
        heights = jax.random.uniform(jax.random.fold_in(jax.random.fold_in(own_key, 6), axis_at), (blocks,), jnp.float32, smallest / len(shards), high / len(shards))
        level = level * jnp.repeat(jnp.exp(heights), shape[axis_at] // blocks).reshape((-1,) + (1,) * (len(shape) - 1 - axis_at))
    return level


def gaussian(stream_key, shape, spread, bound, split=(), held_as=jnp.bfloat16):
    entries = jax.random.normal(stream_key, shape, jnp.float32) * spread
    if len(split) > 0:
        entries = block_levels(stream_key, shape, split, -0.22, 0.18) * entries
    return jnp.clip(entries, min=-bound, max=bound).astype(held_as)


def bell_draw_with(key, dims, scale, limit, shards, heavy, dtype=jnp.bfloat16):
    values = scale * jax.random.normal(key, dims, jnp.float32)
    if shards:
        values = values * block_levels(key, dims, shards, -0.22, 0.18)
    return jnp.clip(spiked(values, jax.random.fold_in(key, 3), *heavy), -limit, limit).astype(dtype)


def setup_inputs(seed: int = 0) -> dict:
    key_list = jax.random.split(jax.random.key(seed), 9)
    inputs = gaussian(key_list[0], (REPLICAS, TOK_REP, D), 1.0, 6.0, ((0, 8), (1, 4)))
    cotangent = gaussian(key_list[1], (REPLICAS, TOK_REP, KVW), 1.0, 6.0, ((0, 8), (1, 4)))
    weight = gaussian(key_list[2], (REPLICAS, D, KVW), D ** -0.5, 0.0625, ((0, 8), (1, 4)))
    adam_first = gaussian(key_list[3], (REPLICAS, D, KVW), (TOK_REP ** -0.5), 0.1875, ((0, 8), (1, 4)))
    adam_second = jnp.clip(jnp.exp(math.log(0.00390625) - 2.7725887 * jax.random.uniform(key_list[4], (REPLICAS, D, KVW), jnp.float32) ** block_levels(key_list[4], (REPLICAS, D, KVW), ((0, 8), (1, 4)), -0.2, 0.2)), 0.00024414062, 0.00390625).astype(jnp.bfloat16)
    outer_frag = gaussian(key_list[5], (FRAG_ROWS, D), 1.0, 6.0, ((0, 4),))
    local_frag = bell_draw_with(key_list[6], (REPLICAS, FRAG_ROWS, D), 1.0, 6.0, ((0, 8), (1, 4)), (0, 2, 8, 2.0))
    momentum = gaussian(key_list[7], (FRAG_ROWS, D), 0.5, 3.0, ((0, 4),), jnp.float32)
    return {"inputs": inputs, "cotangent": cotangent, "weight": weight, "adam_first": adam_first, "adam_second": adam_second, "outer_frag": outer_frag, "local_frag": local_frag, "momentum": momentum}


beta_first = 0.9
beta_second = 0.95
adam_rate = 0.0003
adam_eps = 1e-08
first_fix = 1.0 - 0.9 ** 10
second_fix = 1.0 - 0.95 ** 10
outer_rate = 0.7
nesterov_mu = 0.9

def adam_update(weight_rows, first_moment, second_moment, gradient):
    first = beta_first * first_moment.astype(jnp.float32) + (1.0 - beta_first) * gradient
    second = beta_second * second_moment.astype(jnp.float32) + (1.0 - beta_second) * gradient * gradient
    step_size = first / first_fix / (jnp.sqrt(second / second_fix) + adam_eps)
    updated = weight_rows.astype(jnp.float32) - adam_rate * step_size
    return (updated.astype(jnp.bfloat16), first.astype(jnp.bfloat16), second.astype(jnp.bfloat16))

def replica_step(operands):
    activations, cotangent_rows, weight_rows, first_moment, second_moment = operands
    input_grad = jnp.dot(cotangent_rows, weight_rows.T, preferred_element_type=jnp.float32).astype(jnp.bfloat16)
    act_blocks = activations.reshape(N_FSDP, TOK_DEV, D)
    cot_blocks = cotangent_rows.reshape(N_FSDP, TOK_DEV, KVW)

    def accumulate(total, pair):
        part = jnp.dot(pair[0].T, pair[1], preferred_element_type=jnp.float32).astype(jnp.bfloat16)
        part = lax.optimization_barrier(part)
        return (total + part.astype(jnp.float32), None)
    summed, unused = lax.scan(accumulate, jnp.zeros((D, KVW), jnp.float32), (act_blocks, cot_blocks))
    gradient = summed / TOK_REP
    updated, first, second = adam_update(weight_rows, first_moment, second_moment, gradient)
    return (input_grad, updated, first, second)

def reference(inputs, cotangent, weight, adam_first, adam_second, outer_frag, local_frag, momentum):
    input_grad, new_weight, new_first, new_second = lax.map(replica_step, (inputs, cotangent, weight, adam_first, adam_second))
    outer_wide = outer_frag.astype(jnp.float32)
    deltas = outer_wide[None] - local_frag.astype(jnp.float32)
    delta = lax.optimization_barrier(jnp.sum(deltas, axis=0)) / N_REPLICA
    new_momentum = nesterov_mu * momentum + delta
    new_outer = outer_wide - outer_rate * (delta + nesterov_mu * new_momentum)
    return (input_grad, new_weight, new_first, new_second, new_outer, new_momentum)
```

```python
import functools

import jax
import jax.numpy as jnp
from jax import lax
from jax.experimental import pallas as pl
from jax.experimental.pallas import tpu as pltpu
from jax.sharding import PartitionSpec as P

beta_first = 0.9
beta_second = 0.95
adam_rate = 0.0003
adam_eps = 1e-08
first_fix = 1.0 - 0.9**10
second_fix = 1.0 - 0.95**10
outer_rate = 0.7
nesterov_mu = 0.9

MESH = pl.DeviceIdType.MESH
CHUNK = 256
WINDOW = 3
SUB = 32


def kernel(
    n,
    replicas,
    x_in,
    cot_in,
    w_in,
    m_in,
    v_in,
    outer_in,
    local_in,
    mom_in,
    out_o,
    w_o,
    m_o,
    v_o,
    outer_o,
    mom_o,
    x,
    cot,
    w,
    m,
    v,
    out,
    own,
    held,
    frag,
    outer,
    mom,
    new_outer,
    new_mom,
    load_sem,
    out_sem,
    new_sem,
    frag_out_sem,
    send_sem,
    recv_sem,
    frag_send,
    frag_recv,
):
    me = lax.axis_index("fsdp")
    rep = lax.axis_index("replica")
    rows = w.shape[0]
    chunk = min(CHUNK, rows)
    per = rows // chunk
    tokens = cot.shape[0] * n
    last = n - 1

    loads = [
        pltpu.make_async_copy(src, dst, load_sem.at[k])
        for k, (src, dst) in enumerate(
            [
                (cot_in, cot),
                (w_in, w),
                (x_in, x),
                (outer_in, outer),
                (mom_in, mom),
                (m_in, m),
                (v_in, v),
                (local_in, frag.at[rep]),
            ]
        )
    ]
    for load in loads:
        load.start()

    place = (me, last - me)
    ahead = (jnp.minimum(me + 1, last), jnp.maximum(me - 1, 0))

    barrier = pltpu.get_barrier_semaphore()
    for d in range(2):

        @pl.when(place[d] < last)
        def _():
            pl.semaphore_signal(barrier, inc=1, device_id={"fsdp": ahead[d]}, device_id_type=MESH)

    @pl.loop(1, replicas)
    def _(k):
        peer = lax.rem(rep + k, replicas)
        pl.semaphore_signal(barrier, inc=1, device_id={"replica": peer}, device_id_type=MESH)

    neighbours = jnp.where(me > 0, 1, 0) + jnp.where(me < last, 1, 0)
    pl.semaphore_wait(barrier, replicas - 1 + neighbours)

    def part_rows(c):
        return pl.ds(pl.multiple_of(c * chunk, chunk), chunk)

    def hop(d, t, c, src):
        return pltpu.make_async_remote_copy(
            src_ref=src,
            dst_ref=held.at[d, t, part_rows(c)],
            send_sem=send_sem.at[d, t * per + c],
            recv_sem=recv_sem.at[d, t * per + c],
            device_id={"fsdp": ahead[d]},
            device_id_type=MESH,
        )

    def wait_sent(d, s):
        t, c = s // per, lax.rem(s, per)
        hop(d, t, c, held.at[d, t, part_rows(c)]).wait_send()

    def wait_got(d, t, c):
        hop(d, t, c, held.at[d, t, part_rows(c)]).wait_recv()

    def frag_copy(k, owner):
        return pltpu.make_async_remote_copy(
            src_ref=frag.at[owner],
            dst_ref=frag.at[owner],
            send_sem=frag_send.at[k],
            recv_sem=frag_recv.at[owner],
            device_id={"replica": lax.rem(rep + k, replicas)},
            device_id_type=MESH,
        )

    def columns(owner, c):
        return pl.ds(pl.multiple_of(owner * rows + c * chunk, chunk), chunk)

    def grad_term(owner, c):
        return lax.dot_general(
            x[:, columns(owner, c)],
            cot[...],
            (((0,), (0,)), ((), ())),
            preferred_element_type=jnp.float32,
        )

    def out_copy(owner, c):
        return pltpu.make_async_copy(
            out.at[:, columns(owner, c)], out_o.at[:, columns(owner, c)], out_sem.at[owner, c]
        )

    def out_block(owner, c, block):
        out[:, columns(owner, c)] = lax.dot_general(
            cot[...], block, (((1,), (1,)), ((), ())), preferred_element_type=jnp.float32
        ).astype(out.dtype)
        out_copy(owner, c).start()

    def window(d, s):
        @pl.when(s >= WINDOW)
        def _():
            wait_sent(d, s - WINDOW)

    @pl.loop(0, per)
    def _(c):
        for d in range(2):

            @pl.when(place[d] < last)
            def _():
                window(d, c)
                hop(d, 0, c, w_in.at[part_rows(c)]).start()

        @pl.when(c == 0)
        def _():
            loads[7].wait()

            @pl.loop(1, replicas)
            def _(k):
                frag_copy(k, rep).start()

            for k in range(3):
                loads[k].wait()

        out_block(me, c, w[part_rows(c), :])
        own[part_rows(c), :] = grad_term(me, c)

    loads[3].wait()
    loads[4].wait()

    @pl.loop(1, replicas)
    def _(k):
        frag_copy(k, rep).wait_send()
        frag_copy(k, lax.rem(rep + k, replicas)).wait_recv()

    width = 1024

    @pl.loop(0, outer.shape[1] // width)
    def _(b):
        at = pl.ds(pl.multiple_of(b * width, width), width)
        wide = outer[:, at].astype(jnp.float32)
        total = jnp.zeros_like(wide)
        for q in range(replicas):
            total += wide - frag[q, :, at].astype(jnp.float32)
        delta = total / replicas
        momentum = nesterov_mu * mom[:, at] + delta
        new_mom[:, at] = momentum
        new_outer[:, at] = wide - outer_rate * (delta + nesterov_mu * momentum)

    frag_outs = [
        pltpu.make_async_copy(new_outer, outer_o, frag_out_sem.at[0]),
        pltpu.make_async_copy(new_mom, mom_o, frag_out_sem.at[1]),
    ]
    for copy in frag_outs:
        copy.start()

    @pl.loop(per, n * per)
    def _(s):
        t, c = s // per, lax.rem(s, per)
        for d in range(2):
            slot = held.at[d, t - 1, part_rows(c)]
            is_weight = t <= place[d]

            @pl.when(place[d] > 0)
            def _():
                wait_got(d, t - 1, c)

            @pl.when(jnp.logical_not(is_weight))
            def _():
                target = n + me - t if d == 0 else t + me - n
                term = grad_term(target, c)

                @pl.when(place[d] > 0)
                def _():
                    slot[...] = (slot[...].astype(jnp.float32) + term).astype(slot.dtype)

                @pl.when(place[d] == 0)
                def _():
                    slot[...] = term.astype(slot.dtype)

            @pl.when(place[d] < last)
            def _():
                window(d, s)
                hop(d, t, c, slot).start()

            @pl.when(is_weight)
            def _():
                out_block(me - t if d == 0 else me + t, c, slot[...])

    loads[5].wait()
    loads[6].wait()

    def new_copies(c):
        return [
            pltpu.make_async_copy(src.at[part_rows(c)], dst.at[part_rows(c)], new_sem.at[k, c])
            for k, (src, dst) in enumerate([(w, w_o), (m, m_o), (v, v_o)])
        ]

    @pl.loop(0, per)
    def _(c):
        for d in range(2):

            @pl.when(place[d] > 0)
            def _():
                wait_got(d, last, c)
                own[part_rows(c), :] += held[d, last, part_rows(c), :].astype(jnp.float32)

        @pl.loop(0, chunk // SUB)
        def _(b):
            at = pl.ds(pl.multiple_of(c * chunk + b * SUB, SUB), SUB)
            gradient = own[at, :] / tokens
            first = beta_first * m[at, :].astype(jnp.float32) + (1.0 - beta_first) * gradient
            second = (
                beta_second * v[at, :].astype(jnp.float32)
                + (1.0 - beta_second) * gradient * gradient
            )
            step_size = first / first_fix / (jnp.sqrt(second / second_fix) + adam_eps)
            w[at, :] = (w[at, :].astype(jnp.float32) - adam_rate * step_size).astype(w.dtype)
            m[at, :] = first.astype(m.dtype)
            v[at, :] = second.astype(v.dtype)

        for copy in new_copies(c):
            copy.start()

    for d in range(2):

        @pl.when(place[d] < last)
        def _():
            @pl.loop(n * per - WINDOW, n * per)
            def _(s):
                wait_sent(d, s)

    @pl.loop(0, n * per)
    def _(s):
        out_copy(s // per, lax.rem(s, per)).wait()

    for copy in frag_outs:
        copy.wait()

    @pl.loop(0, per)
    def _(c):
        for copy in new_copies(c):
            copy.wait()


def on_device(inputs, cotangent, weight, adam_first, adam_second, outer_frag, local_frag, momentum):
    n = lax.axis_size("fsdp")
    replicas = lax.axis_size("replica")
    x, cot, w, m, v, local = (
        inputs[0],
        cotangent[0],
        weight[0],
        adam_first[0],
        adam_second[0],
        local_frag[0],
    )
    rows, features = w.shape
    tokens, model = x.shape
    per = rows // min(CHUNK, rows)
    bf16, f32 = jnp.bfloat16, jnp.float32
    shape = jax.ShapeDtypeStruct
    anywhere = pl.BlockSpec(memory_space=pl.ANY)
    dma = pltpu.SemaphoreType.DMA
    results = pl.pallas_call(
        functools.partial(kernel, n, replicas),
        out_shape=(
            shape((tokens, model), bf16),
            shape(w.shape, bf16),
            shape(w.shape, bf16),
            shape(w.shape, bf16),
            shape(momentum.shape, f32),
            shape(momentum.shape, f32),
        ),
        in_specs=[anywhere] * 8,
        out_specs=[anywhere] * 6,
        scratch_shapes=[
            pltpu.VMEM((tokens, model), bf16),
            pltpu.VMEM((tokens, features), bf16),
            pltpu.VMEM(w.shape, bf16),
            pltpu.VMEM(w.shape, bf16),
            pltpu.VMEM(w.shape, bf16),
            pltpu.VMEM((tokens, model), bf16),
            pltpu.VMEM(w.shape, f32),
            pltpu.VMEM((2, n, rows, features), bf16),
            pltpu.VMEM((replicas,) + local.shape, bf16),
            pltpu.VMEM(outer_frag.shape, bf16),
            pltpu.VMEM(momentum.shape, f32),
            pltpu.VMEM(momentum.shape, f32),
            pltpu.VMEM(momentum.shape, f32),
            dma((8,)),
            dma((n, per)),
            dma((3, per)),
            dma((2,)),
            dma((2, n * per)),
            dma((2, n * per)),
            dma((replicas,)),
            dma((replicas,)),
        ],
        compiler_params=pltpu.CompilerParams(
            collective_id=0, has_side_effects=True, vmem_limit_bytes=48 * 1024 * 1024
        ),
        cost_estimate=pl.CostEstimate(
            flops=4 * tokens * model * features,
            bytes_accessed=4 * tokens * model + 12 * rows * features,
            transcendentals=rows * features,
        ),
    )(x, cot, w, m, v, outer_frag, local, momentum)
    input_grad, updated, first, second, new_outer, new_momentum = results
    return (input_grad[None], updated[None], first[None], second[None], new_outer, new_momentum)


def solution(mesh):
    return jax.shard_map(
        on_device,
        mesh=mesh,
        in_specs=(
            P("replica", "fsdp", None),
            P("replica", "fsdp", None),
            P("replica", "fsdp", None),
            P("replica", "fsdp", None),
            P("replica", "fsdp", None),
            P("fsdp", None),
            P("replica", "fsdp", None),
            P("fsdp", None),
        ),
        out_specs=(
            P("replica", "fsdp", None),
            P("replica", "fsdp", None),
            P("replica", "fsdp", None),
            P("replica", "fsdp", None),
            P("fsdp", None),
            P("fsdp", None),
        ),
        check_vma=False,
    )
```

```python
import functools

import jax
import jax.numpy as jnp
from jax import lax
from jax.experimental import pallas as pl
from jax.experimental.pallas import tpu as pltpu
from jax.sharding import PartitionSpec as P

beta_first = 0.9
beta_second = 0.95
adam_rate = 0.0003
adam_eps = 1e-08
first_fix = 1.0 - 0.9**10
second_fix = 1.0 - 0.95**10
outer_rate = 0.7
nesterov_mu = 0.9

MESH = pl.DeviceIdType.MESH
CHUNK = 256
WINDOW = 3
SUB = 32


def kernel(
    n,
    replicas,
    x_in,
    cot_in,
    w_in,
    m_in,
    v_in,
    outer_in,
    local_in,
    mom_in,
    out,
    w,
    m,
    v,
    new_outer,
    new_mom,
    x,
    cot,
    own,
    held,
    frag,
    outer,
    mom,
    load_sem,
    send_sem,
    recv_sem,
    frag_send,
    frag_recv,
):
    me = lax.axis_index("fsdp")
    rep = lax.axis_index("replica")
    rows = w.shape[0]
    chunk = min(CHUNK, rows)
    per = rows // chunk
    tokens = cot.shape[0] * n
    last = n - 1

    loads = [
        pltpu.make_async_copy(src, dst, load_sem.at[k])
        for k, (src, dst) in enumerate(
            [
                (cot_in, cot),
                (w_in, w),
                (x_in, x),
                (outer_in, outer),
                (mom_in, mom),
                (m_in, m),
                (v_in, v),
                (local_in, frag.at[rep]),
            ]
        )
    ]
    for load in loads:
        load.start()

    place = (me, last - me)
    ahead = (jnp.minimum(me + 1, last), jnp.maximum(me - 1, 0))

    barrier = pltpu.get_barrier_semaphore()
    for d in range(2):

        @pl.when(place[d] < last)
        def _():
            pl.semaphore_signal(barrier, inc=1, device_id={"fsdp": ahead[d]}, device_id_type=MESH)

    @pl.loop(1, replicas)
    def _(k):
        peer = lax.rem(rep + k, replicas)
        pl.semaphore_signal(barrier, inc=1, device_id={"replica": peer}, device_id_type=MESH)

    neighbours = jnp.where(me > 0, 1, 0) + jnp.where(me < last, 1, 0)
    pl.semaphore_wait(barrier, replicas - 1 + neighbours)

    def part_rows(c):
        return pl.ds(pl.multiple_of(c * chunk, chunk), chunk)

    def hop(d, t, c, src):
        return pltpu.make_async_remote_copy(
            src_ref=src,
            dst_ref=held.at[d, t, part_rows(c)],
            send_sem=send_sem.at[d, t * per + c],
            recv_sem=recv_sem.at[d, t * per + c],
            device_id={"fsdp": ahead[d]},
            device_id_type=MESH,
        )

    def wait_sent(d, s):
        t, c = s // per, lax.rem(s, per)
        hop(d, t, c, held.at[d, t, part_rows(c)]).wait_send()

    def wait_got(d, t, c):
        hop(d, t, c, held.at[d, t, part_rows(c)]).wait_recv()

    def frag_copy(k, owner):
        return pltpu.make_async_remote_copy(
            src_ref=frag.at[owner],
            dst_ref=frag.at[owner],
            send_sem=frag_send.at[k],
            recv_sem=frag_recv.at[owner],
            device_id={"replica": lax.rem(rep + k, replicas)},
            device_id_type=MESH,
        )

    def columns(owner, c):
        return pl.ds(pl.multiple_of(owner * rows + c * chunk, chunk), chunk)

    def grad_term(owner, c):
        return lax.dot_general(
            x[:, columns(owner, c)],
            cot[...],
            (((0,), (0,)), ((), ())),
            preferred_element_type=jnp.float32,
        )

    def out_block(owner, c, block):
        out[:, columns(owner, c)] = lax.dot_general(
            cot[...], block, (((1,), (1,)), ((), ())), preferred_element_type=jnp.float32
        ).astype(out.dtype)

    def window(d, s):
        @pl.when(s >= WINDOW)
        def _():
            wait_sent(d, s - WINDOW)

    @pl.loop(0, per)
    def _(c):
        for d in range(2):

            @pl.when(place[d] < last)
            def _():
                window(d, c)
                hop(d, 0, c, w_in.at[part_rows(c)]).start()

        @pl.when(c == 0)
        def _():
            loads[7].wait()

            @pl.loop(1, replicas)
            def _(k):
                frag_copy(k, rep).start()

            for k in range(3):
                loads[k].wait()

        out_block(me, c, w[part_rows(c), :])
        own[part_rows(c), :] = grad_term(me, c)

    loads[3].wait()
    loads[4].wait()

    @pl.loop(1, replicas)
    def _(k):
        frag_copy(k, rep).wait_send()
        frag_copy(k, lax.rem(rep + k, replicas)).wait_recv()

    width = 1024

    @pl.loop(0, outer.shape[1] // width)
    def _(b):
        at = pl.ds(pl.multiple_of(b * width, width), width)
        wide = outer[:, at].astype(jnp.float32)
        total = jnp.zeros_like(wide)
        for q in range(replicas):
            total += wide - frag[q, :, at].astype(jnp.float32)
        delta = total / replicas
        momentum = nesterov_mu * mom[:, at] + delta
        new_mom[:, at] = momentum
        new_outer[:, at] = wide - outer_rate * (delta + nesterov_mu * momentum)

    @pl.loop(per, n * per)
    def _(s):
        t, c = s // per, lax.rem(s, per)
        for d in range(2):
            slot = held.at[d, t - 1, part_rows(c)]
            is_weight = t <= place[d]

            @pl.when(place[d] > 0)
            def _():
                wait_got(d, t - 1, c)

            @pl.when(jnp.logical_not(is_weight))
            def _():
                target = n + me - t if d == 0 else t + me - n
                term = grad_term(target, c)

                @pl.when(place[d] > 0)
                def _():
                    slot[...] = (slot[...].astype(jnp.float32) + term).astype(slot.dtype)

                @pl.when(place[d] == 0)
                def _():
                    slot[...] = term.astype(slot.dtype)

            @pl.when(place[d] < last)
            def _():
                window(d, s)
                hop(d, t, c, slot).start()

            @pl.when(is_weight)
            def _():
                out_block(me - t if d == 0 else me + t, c, slot[...])

    loads[5].wait()
    loads[6].wait()

    @pl.loop(0, per)
    def _(c):
        for d in range(2):

            @pl.when(place[d] > 0)
            def _():
                wait_got(d, last, c)
                own[part_rows(c), :] += held[d, last, part_rows(c), :].astype(jnp.float32)

        @pl.loop(0, chunk // SUB)
        def _(b):
            at = pl.ds(pl.multiple_of(c * chunk + b * SUB, SUB), SUB)
            gradient = own[at, :] / tokens
            first = beta_first * m[at, :].astype(jnp.float32) + (1.0 - beta_first) * gradient
            second = (
                beta_second * v[at, :].astype(jnp.float32)
                + (1.0 - beta_second) * gradient * gradient
            )
            step_size = first / first_fix / (jnp.sqrt(second / second_fix) + adam_eps)
            w[at, :] = (w[at, :].astype(jnp.float32) - adam_rate * step_size).astype(w.dtype)
            m[at, :] = first.astype(m.dtype)
            v[at, :] = second.astype(v.dtype)

    for d in range(2):

        @pl.when(place[d] < last)
        def _():
            @pl.loop(n * per - WINDOW, n * per)
            def _(s):
                wait_sent(d, s)


def write_kernel(*refs):
    count = (len(refs) - 1) // 2
    copies = [
        pltpu.make_async_copy(refs[k], refs[count + k], refs[-1].at[k]) for k in range(count)
    ]
    for copy in copies:
        copy.start()
    for copy in copies:
        copy.wait()


def on_device(inputs, cotangent, weight, adam_first, adam_second, outer_frag, local_frag, momentum):
    n = lax.axis_size("fsdp")
    replicas = lax.axis_size("replica")
    x, cot, w, m, v, local = (
        inputs[0],
        cotangent[0],
        weight[0],
        adam_first[0],
        adam_second[0],
        local_frag[0],
    )
    rows, features = w.shape
    tokens, model = x.shape
    per = rows // min(CHUNK, rows)
    bf16, f32 = jnp.bfloat16, jnp.float32
    shape = jax.ShapeDtypeStruct
    hbm, vmem = pl.BlockSpec(memory_space=pltpu.HBM), pl.BlockSpec(memory_space=pltpu.VMEM)
    dma = pltpu.SemaphoreType.DMA
    kinds = [
        ((tokens, model), bf16),
        (w.shape, bf16),
        (w.shape, bf16),
        (w.shape, bf16),
        (momentum.shape, f32),
        (momentum.shape, f32),
    ]
    results = pl.pallas_call(
        functools.partial(kernel, n, replicas),
        out_shape=[pltpu.VMEM(*kind) for kind in kinds],
        in_specs=[hbm] * 8,
        out_specs=[vmem] * 6,
        scratch_shapes=[
            pltpu.VMEM((tokens, model), bf16),
            pltpu.VMEM((tokens, features), bf16),
            pltpu.VMEM(w.shape, f32),
            pltpu.VMEM((2, n, rows, features), bf16),
            pltpu.VMEM((replicas,) + local.shape, bf16),
            pltpu.VMEM(outer_frag.shape, bf16),
            pltpu.VMEM(momentum.shape, f32),
            dma((8,)),
            dma((2, n * per)),
            dma((2, n * per)),
            dma((replicas,)),
            dma((replicas,)),
        ],
        compiler_params=pltpu.CompilerParams(
            collective_id=0, has_side_effects=True, vmem_limit_bytes=40 * 1024 * 1024
        ),
        cost_estimate=pl.CostEstimate(
            flops=4 * tokens * model * features,
            bytes_accessed=4 * tokens * model + 12 * rows * features,
            transcendentals=rows * features,
        ),
    )(*[
        pltpu.with_memory_space_constraint(a, pltpu.HBM)
        for a in (x, cot, w, m, v, outer_frag, local, momentum)
    ])
    results = pl.pallas_call(
        write_kernel,
        out_shape=[shape(*kind) for kind in kinds],
        in_specs=[pl.BlockSpec(memory_space=pl.ANY)] * 6,
        out_specs=[hbm] * 6,
        scratch_shapes=[dma((6,))],
        compiler_params=pltpu.CompilerParams(vmem_limit_bytes=1024 * 1024),
    )(*[pltpu.with_memory_space_constraint(a, pltpu.VMEM) for a in results])
    input_grad, updated, first, second, new_outer, new_momentum = results
    return (input_grad[None], updated[None], first[None], second[None], new_outer, new_momentum)


def solution(mesh):
    return jax.shard_map(
        on_device,
        mesh=mesh,
        in_specs=(
            P("replica", "fsdp", None),
            P("replica", "fsdp", None),
            P("replica", "fsdp", None),
            P("replica", "fsdp", None),
            P("replica", "fsdp", None),
            P("fsdp", None),
            P("replica", "fsdp", None),
            P("fsdp", None),
        ),
        out_specs=(
            P("replica", "fsdp", None),
            P("replica", "fsdp", None),
            P("replica", "fsdp", None),
            P("replica", "fsdp", None),
            P("fsdp", None),
            P("fsdp", None),
        ),
        check_vma=False,
    )
```
